512 devices in a mesh: grp: 8 (over y), sub: 64 (over z, x, core).
Axes of the slice: x: 4, y: 8, z: 8, core: 2. Of those that a mesh axis runs over, the one named last changes fastest.
Arguments:
- right_sides: float32 [262144, 128], P(('grp', 'sub')), may hold values from -6 to 6
- basis_u: bfloat16 [5, 262144, 256], P(None, ('grp', 'sub')), may hold values from -0.15625 to 0.15625
- basis_v: bfloat16 [5, 262144, 256], P(None, ('grp', 'sub')), may hold values from -0.25 to 0.25
- coupling: bfloat16 [5, 131072, 512], P(None, ('grp', 'sub')), may hold values from -0.03314563 to 0.03314563, as said below
Outputs:
- solution: float32 [262144, 128], P(('grp', 'sub'))
The draws below stay inside these ranges and needn't reach their ends.
Inputs may be any that keep to these rules, and one draw needn't show every extreme that they name: For level l the 256 rows of coupling on a device equal those on every device whose index (grp major) agrees with it in all bits from bit 9 - 5 + l upwards. Entries of level l are independent, of mean 0 and deviation (2 * 256 * 2**(4 + l))**-0.5, and lie within three such deviations.
All inputs are finite; a program needn't handle non-finite values.
Results may differ from the reference program's by a relative error of at most 0.0003.
Values sent between devices are 32-bit elements; how exact they have to be, the bound alone decides.
A program may use at most 64 MiB of HBM per device.

```python
import jax
import jax.numpy as jnp
from jax import lax

RANK = 256
PTS_DEV = 512
COLS = 128
LEVELS = 5
BITS = 9
ROWS = 262144
N_GRP = 8
N_SUB = 64


def draw_coupling(key, part):
    key = jax.random.fold_in(key, 11)
    devices = N_GRP * N_SUB
    blocks = []
    for height in range(LEVELS):
        span_bits = BITS - LEVELS + height
        group_ids = jnp.arange(devices) // 2 ** span_bits
        level_key = jax.random.fold_in(key, height)
        keys = jax.vmap(lambda group: jax.random.fold_in(level_key, group))(group_ids)
        scale = (2.0 * RANK * 2 ** span_bits) ** (-0.5)
        values = jax.vmap(lambda one: jnp.clip(jax.random.normal(one, (RANK, 2 * RANK), jnp.float32), -2.99, 2.99))(keys)
        blocks.append((values * scale).reshape(devices * RANK, 2 * RANK).astype(jnp.bfloat16))
    return jnp.stack(blocks)


def block_levels(own_key, shape, cuts, low, top_value):
    def one(dim, blocks):
        draws = jax.random.uniform(jax.random.fold_in(jax.random.fold_in(own_key, 6), dim), (blocks,), jnp.float32, low / len(cuts), top_value / len(cuts))
        return jnp.repeat(jnp.exp(draws), shape[dim] // blocks).reshape((-1,) + (1,) * (len(shape) - dim - 1))

    level = one(*cuts[0])
    for cut in cuts[1:]:
        level = level * one(*cut)
    return level


def scatter_about(own_key, extent, deviation, bound, shards=(), kind=jnp.bfloat16):
    level = block_levels(own_key, extent, shards, -0.22, 0.18) if shards else 1.0
    array = jax.random.normal(own_key, extent, jnp.float32) * deviation * level
    return jnp.minimum(jnp.maximum(array, -bound), bound).astype(kind)


def setup_inputs(seed: int = 0) -> dict:
    arg_keys = jax.random.split(jax.random.key(seed), 5)
    right_sides = scatter_about(arg_keys[0], (ROWS, COLS), 1.0, 6.0, ((0, 512),), jnp.float32)
    basis_u = scatter_about(arg_keys[1], (LEVELS, ROWS, RANK), (RANK * LEVELS) ** -0.5, 0.15625, ((1, 512),))
    basis_v = scatter_about(arg_keys[2], (LEVELS, ROWS, RANK), PTS_DEV ** -0.5, 0.25, ((1, 512),))
    coupling = draw_coupling(jax.random.fold_in(arg_keys[4], 71), 0)
    return {"right_sides": right_sides, "basis_u": basis_u, "basis_v": basis_v, "coupling": coupling}


def reference(right_sides, basis_u, basis_v, coupling):
    devices = N_GRP * N_SUB
    highest = lax.Precision.HIGHEST
    current = right_sides.reshape(devices, PTS_DEV, COLS)
    for height in range(LEVELS):
        span_bits = BITS - LEVELS + height
        v_basis = basis_v[height].astype(jnp.float32).reshape(devices, PTS_DEV, RANK)
        u_basis = basis_u[height].astype(jnp.float32).reshape(devices, PTS_DEV, RANK)
        couple_rows = coupling[height].astype(jnp.float32).reshape(devices, RANK, 2 * RANK)
        partial_value = jnp.einsum("dpr,dpn->drn", v_basis, current, precision=highest)
        group_sums = partial_value.reshape(devices // (2 ** span_bits), 2 ** span_bits, RANK, COLS).sum(axis=1)
        node_sums = group_sums.reshape(devices // (2 ** (span_bits + 1)), 2 * RANK, COLS)
        spread = jnp.repeat(node_sums, 2 ** (span_bits + 1), axis=0)
        weights = jnp.einsum("drs,dsn->drn", couple_rows, spread, precision=highest)
        current = current - jnp.einsum("dpr,drn->dpn", u_basis, weights, precision=highest)
    return current.reshape(devices * PTS_DEV, COLS)
```

```python
import functools

import jax
import jax.numpy as jnp
from jax import lax
from jax.experimental import pallas as pl
from jax.experimental.pallas import tpu as pltpu
from jax.sharding import PartitionSpec as P

F32 = jnp.float32
BF16 = jnp.bfloat16
RANK = 256
PTS = 512
COLS = 128
LEVELS = 5
SEMS = 224
SL = 8
XS = 16
XA = ((2, 1), (3, 1), (4, 1))
XB = ((3, 2), (4, 2), (4, 3))


def split2(a):
    hi = a.astype(BF16)
    lo = (a - hi.astype(F32)).astype(BF16)
    return hi, lo


def stacked(a):
    hi = a.astype(BF16).astype(F32)
    return jnp.concatenate([hi, a - hi], axis=0).astype(BF16)


def mm(a, b):
    return lax.dot_general(a, b, (((1,), (0,)), ((), ())), preferred_element_type=F32)


def mm_t(a, b):
    return lax.dot_general(a, b, (((1,), (1,)), ((), ())), preferred_element_type=F32)


def halves(a):
    n = a.shape[0] // 2
    return a[:n] + a[n:]


def kernel(rs_hbm, u_hbm, v_hbm, c_hbm, out_ref, r0, u, v, cpl, cur_t,
           l0, rc0, r0s, l1, rc1, r1s, la, rca, ras, lb, rcb, rbs,
           sla, slb, zar, zbr, ybr, xa, xb, xah, xal, xbh, xbl,
           p0, q0r, p1, q1p, q1s, p2, q2p, q2s, p3, q3p, q3s, p4, q4p,
           wown, wall, ld, ss, rs):
    y = lax.axis_index("grp")
    s = lax.axis_index("sub")
    core = s % 2
    chip = (s // 2) % 8
    plane = s // 16
    lane = s % 16
    base = s - lane

    def near(k):
        return (y, base + (lane + k) % 16)

    def same_core(k):
        return (y, base + 2 * ((chip + k) % 8) + core)

    other_core = (y, s + 1 - 2 * core)
    plane_by = {1: plane + 1 - 2 * (plane % 2), 2: (plane + 2) % 4, 3: 3 - plane}
    y2 = y + 2 - 4 * ((y // 2) % 2)
    y_by = {1: y + 1 - 2 * (y % 2), 2: y2, 3: 4 * (y // 4) + 3 - y % 4, 4: (y + 4) % 8, 6: (y2 + 4) % 8}

    def far(zmask, ymask):
        ss_ = s + 16 * (plane_by[zmask] - plane) if zmask else s
        return (y_by[ymask] if ymask else y, ss_)

    far_masks = [(1, 0), (2, 0), (3, 0), (0, 1), (2, 1), (0, 2), (0, 3), (0, 4), (0, 6)]
    MESH = pl.DeviceIdType.MESH
    barrier = pltpu.get_barrier_semaphore()
    for m in far_masks:
        pl.semaphore_signal(barrier, inc=1, device_id=far(*m), device_id_type=MESH)
    for k in range(1, 16):
        pl.semaphore_signal(barrier, inc=1, device_id=near(k), device_id_type=MESH)

    loads = {}

    def load(name, src, dst):
        loads[name] = pltpu.make_async_copy(src, dst, ld.at[len(loads)])
        loads[name].start()

    load("r", rs_hbm, r0)
    load("v0", v_hbm.at[0], v.at[0])
    load("u1", u_hbm.at[1], u.at[1])
    for m in (2, 3, 4):
        load("v%d" % m, v_hbm.at[m], v.at[m])
    load("c0", c_hbm.at[0], cpl.at[0])
    load("u2", u_hbm.at[2], u.at[2])
    load("u3", u_hbm.at[3], u.at[3])
    load("u0", u_hbm.at[0], u.at[0])
    load("v1", v_hbm.at[1], v.at[1])
    for m in (1, 2, 3, 4):
        load("c%d" % m, c_hbm.at[m], cpl.at[m])
    load("u4", u_hbm.at[4], u.at[4])

    pending = []
    count = [0]

    def send(src, dst, device):
        i = count[0]
        count[0] += 1
        cp = pltpu.make_async_remote_copy(src_ref=src, dst_ref=dst, send_sem=ss.at[i], recv_sem=rs.at[i],
                                          device_id=device, device_id_type=MESH)
        cp.start()
        pending.append(cp)
        return cp

    def flush():
        for cp in pending:
            cp.wait_send()
        pending.clear()

    def core_send(l, rc):
        return send(l.at[1 - core], rc, other_core)

    def core_add(cp, l, rc):
        cp.wait_recv()
        rc[...] = rc[...] + l[core]

    def rs_send(rc, slots):
        return [send(rc.at[(chip + k) % 8], slots.at[k - 1], same_core(k)) for k in range(1, 8)]

    def rs_sum(cps, rc, slots):
        for cp in cps:
            cp.wait_recv()
        total = rc[chip]
        for k in range(7):
            total = total + slots[k]
        return total

    def ag_send(src, full, first=None, size=None):
        out = []
        for k in range(1, 8):
            def at(i):
                return full.at[core, i] if first is None else full.at[core, i, pl.ds(first, size)]
            cp = send(src, at(chip), same_core(k))
            arrive = pltpu.make_async_remote_copy(src_ref=src, dst_ref=at((chip + 8 - k) % 8), send_sem=ss.at[count[0] - 1],
                                                  recv_sem=rs.at[count[0] - 1], device_id=same_core(k), device_id_type=MESH)
            out.append(arrive)
        return out

    def share_send(cps, full):
        for cp in cps:
            cp.wait_recv()
        cp = send(full.at[core], full.at[core], other_core)
        return pltpu.make_async_remote_copy(src_ref=full.at[core], dst_ref=full.at[1 - core], send_sem=ss.at[count[0] - 1],
                                            recv_sem=rs.at[count[0] - 1], device_id=other_core, device_id_type=MESH)

    def w_send(level, value):
        wown[level] = value
        wall[level, core * 8 + chip] = value
        out = []
        for k in range(1, 16):
            send(wown.at[level], wall.at[level, core * 8 + chip], near(k))
            frm = (lane + 16 - k) % 16
            i = count[0] - 1
            out.append(pltpu.make_async_remote_copy(
                src_ref=wown.at[level], dst_ref=wall.at[level, (frm % 2) * 8 + frm // 2], send_sem=ss.at[i],
                recv_sem=rs.at[i], device_id=near(k), device_id_type=MESH))
        return out

    def w_full(level, cps):
        for cp in cps:
            cp.wait_recv()
        return stacked(wall[level].reshape(COLS, RANK))

    def weights(level, own, sibling, upper):
        loads["c%d" % level].wait()
        first = jnp.where(upper == 0, own, sibling)
        second = jnp.where(upper == 0, sibling, own)
        node = jnp.concatenate([first, second], axis=1)
        return halves(mm_t(stacked(node), cpl[level]))

    def slices(value, n):
        return value.reshape(2, 8, n, RANK)

    loads["r"].wait()
    rt = r0[...].T
    cur_t[...] = rt
    loads["v0"].wait()
    l0[...] = slices(halves(mm(stacked(rt), v[0])), SL)
    pl.semaphore_wait(barrier, len(far_masks) + 15)
    c_0 = core_send(l0, rc0)
    loads["u1"].wait()
    ut = u[1].T
    for i, m in enumerate((2, 3, 4)):
        loads["v%d" % m].wait()
        la[:, :, i * XS:(i + 1) * XS, :] = slices(mm(ut, v[m]), XS)
    core_add(c_0, l0, rc0)
    g_0 = rs_send(rc0, r0s)
    c_a = core_send(la, rca)
    loads["u2"].wait()
    ut = u[2].T
    for i, m in enumerate((3, 4)):
        lb[:, :, i * XS:(i + 1) * XS, :] = slices(mm(ut, v[m]), XS)
    loads["u3"].wait()
    ut = u[3].T
    lb[:, :, 2 * XS:3 * XS, :] = slices(mm(ut, v[4]), XS)
    c_b = core_send(lb, rcb)

    p0[...] = rs_sum(g_0, rc0, r0s)
    e_0 = send(p0, q0r, far(1, 0))
    core_add(c_a, la, rca)
    g_a = rs_send(rca, ras)
    core_add(c_b, lb, rcb)
    g_b = rs_send(rcb, rbs)
    bit4, bit5 = plane % 2, plane // 2
    e_0.wait_recv()
    w_cps = {}
    w_cps[0] = w_send(0, weights(0, p0[...], q0r[...], bit4))

    sla[...] = rs_sum(g_a, rca, ras)
    z_a = send(sla, zar, far(1, 0))

    loads["u0"].wait()
    w0 = w_full(0, w_cps[0])
    cur = cur_t[...] - halves(mm_t(w0, u[0]))
    cur_s = stacked(cur)
    loads["v1"].wait()
    for m in (1, 2, 3, 4):
        l1[:, :, (m - 1) * SL:m * SL, :] = slices(halves(mm(cur_s, v[m])), SL)
    c_1 = core_send(l1, rc1)
    slb[...] = rs_sum(g_b, rcb, rbs)
    z_b = [send(slb, zbr.at[i], far(i + 1, 0)) for i in range(3)]
    z_a.wait_recv()
    sla_sum = sla[...] + zar[...]
    xa[core, chip] = sla_sum
    a_a = ag_send(xa.at[core, chip], xa)
    core_add(c_1, l1, rc1)
    g_1 = rs_send(rc1, r1s)
    acc = r0[...]
    upd = mm_t(u[0], w0)
    out_ref[...] = acc - (upd[:, :COLS] + upd[:, COLS:])
    flush()
    for cp in z_b:
        cp.wait_recv()
    slb_sum = slb[...] + zbr[0] + (zbr[1] + zbr[2])
    xb[core, chip] = slb_sum
    y_b = send(xb.at[core, chip, pl.ds(2 * XS, XS)], ybr, far(0, 1))
    a_b = ag_send(xb.at[core, chip, pl.ds(0, 2 * XS)], xb, 0, 2 * XS)

    p1[...] = rs_sum(g_1, rc1, r1s)
    e_1 = [send(p1.at[pl.ds(0, SL)], q1p.at[i], far(i + 1, 0)) for i in range(3)]
    e_1s = send(p1.at[pl.ds(SL, 3 * SL)], q1s, far(1, 0))
    s_a = share_send(a_a, xa)
    y_b.wait_recv()
    y_b.wait_send()
    pending.remove(y_b)
    xb[core, chip, pl.ds(2 * XS, XS)] = xb[core, chip, pl.ds(2 * XS, XS)] + ybr[...]
    a_c = ag_send(xb.at[core, chip, pl.ds(2 * XS, XS)], xb, 2 * XS, XS)
    s_a.wait_recv()
    for i in range(3):
        hi, lo = split2(xa[:, :, i * XS:(i + 1) * XS, :].reshape(RANK, RANK))
        xah[i], xal[i] = hi, lo

    def product(w_s, hi, lo):
        return halves(mm(w_s, hi)) + mm(w_s, lo)[:SL]

    for cp in e_1:
        cp.wait_recv()
    w = weights(1, p1[0:SL] + q1p[0], q1p[1] + q1p[2], bit5)
    w_cps[1] = w_send(1, w)
    e_1s.wait_recv()
    ws = stacked(w)
    rest = p1[SL:4 * SL] + q1s[...]
    for i in range(3):
        p2[i * SL:(i + 1) * SL] = rest[i * SL:(i + 1) * SL] - product(ws, xah[i], xal[i])
    peers = [(2, 0), (0, 1), (2, 1)]
    e_2 = [send(p2.at[pl.ds(0, SL)], q2p.at[i], far(*peers[i])) for i in range(3)]
    e_2s = send(p2.at[pl.ds(SL, 2 * SL)], q2s, far(2, 0))
    s_b = share_send(a_b + a_c, xb)
    flush()

    def apply(level):
        ws_ = w_full(level, w_cps[level])
        loads["u%d" % level].wait() if level == 4 else None
        upd_ = mm_t(u[level], ws_)
        out_ref[...] = out_ref[...] - (upd_[:, :COLS] + upd_[:, COLS:])

    apply(1)
    s_b.wait_recv()
    for i in range(3):
        hi, lo = split2(xb[:, :, i * XS:(i + 1) * XS, :].reshape(RANK, RANK))
        xbh[i], xbl[i] = hi, lo

    for cp in e_2:
        cp.wait_recv()
    w = weights(2, p2[0:SL] + q2p[0], q2p[1] + q2p[2], y % 2)
    w_cps[2] = w_send(2, w)
    e_2s.wait_recv()
    ws = stacked(w)
    rest = p2[SL:3 * SL] + q2s[...]
    for i in range(2):
        p3[i * SL:(i + 1) * SL] = rest[i * SL:(i + 1) * SL] - product(ws, xbh[i], xbl[i])
    e_3 = [send(p3.at[pl.ds(0, SL)], q3p.at[i], far(0, i + 1)) for i in range(3)]
    e_3s = send(p3.at[pl.ds(SL, SL)], q3s, far(0, 1))
    flush()
    apply(2)

    for cp in e_3:
        cp.wait_recv()
    w = weights(3, p3[0:SL] + q3p[0], q3p[1] + q3p[2], (y // 2) % 2)
    w_cps[3] = w_send(3, w)
    e_3s.wait_recv()
    p4[...] = p3[SL:2 * SL] + q3s[...] - product(stacked(w), xbh[2], xbl[2])
    ymask = (2, 4, 6)
    e_4 = [send(p4, q4p.at[i], far(0, ymask[i])) for i in range(3)]
    flush()
    apply(3)

    for cp in e_4:
        cp.wait_recv()
    w = weights(4, p4[...] + q4p[0], q4p[1] + q4p[2], y // 4)
    w_cps[4] = w_send(4, w)
    apply(4)
    flush()


def per_device(right_sides, basis_u, basis_v, coupling):
    def vm(*shape, dtype=F32):
        return pltpu.VMEM(shape, dtype)

    scratch = [
        vm(PTS, COLS), vm(LEVELS, PTS, RANK, dtype=BF16), vm(LEVELS, PTS, RANK, dtype=BF16),
        vm(LEVELS, RANK, 2 * RANK, dtype=BF16), vm(COLS, PTS),
    ]
    for n in (SL, 4 * SL, 3 * XS, 3 * XS):
        scratch += [vm(2, 8, n, RANK), vm(8, n, RANK), vm(7, n, RANK)]
    scratch += [
        vm(3 * XS, RANK), vm(3 * XS, RANK), vm(3 * XS, RANK), vm(3, 3 * XS, RANK), vm(XS, RANK),
        vm(2, 8, 3 * XS, RANK), vm(2, 8, 3 * XS, RANK),
    ]
    scratch += [vm(3, RANK, RANK, dtype=BF16)] * 4
    scratch += [
        vm(SL, RANK), vm(SL, RANK),
        vm(4 * SL, RANK), vm(3, SL, RANK), vm(3 * SL, RANK),
        vm(3 * SL, RANK), vm(3, SL, RANK), vm(2 * SL, RANK),
        vm(2 * SL, RANK), vm(3, SL, RANK), vm(SL, RANK),
        vm(SL, RANK), vm(3, SL, RANK),
        vm(LEVELS, SL, RANK), vm(LEVELS, 16, SL, RANK),
        pltpu.SemaphoreType.DMA((16,)), pltpu.SemaphoreType.DMA((SEMS,)), pltpu.SemaphoreType.DMA((SEMS,)),
    ]
    return pl.pallas_call(
        kernel,
        out_shape=jax.ShapeDtypeStruct((PTS, COLS), F32),
        in_specs=[pl.BlockSpec(memory_space=pltpu.HBM)] * 4,
        out_specs=pl.BlockSpec(memory_space=pltpu.VMEM),
        scratch_shapes=scratch,
        compiler_params=pltpu.CompilerParams(collective_id=0, has_side_effects=True, vmem_limit_bytes=48 * 2**20),
        name="hodlr_solve",
    )(right_sides, basis_u, basis_v, coupling)


def solution(mesh):
    in_specs = (
        P(("grp", "sub"), None),
        P(None, ("grp", "sub"), None),
        P(None, ("grp", "sub"), None),
        P(None, ("grp", "sub"), None),
    )
    out_specs = P(("grp", "sub"), None)
    return jax.shard_map(
        per_device, mesh=mesh, in_specs=in_specs, out_specs=out_specs, check_vma=False
    )
```

```python
import functools

import jax
import jax.numpy as jnp
from jax import lax
from jax.experimental import pallas as pl
from jax.experimental.pallas import tpu as pltpu
from jax.sharding import PartitionSpec as P

F32 = jnp.float32
BF16 = jnp.bfloat16
RANK = 256
PTS = 512
COLS = 128
LEVELS = 5
SEMS = 32
SL = 8
XS = 16


def split2(a):
    hi = a.astype(BF16)
    lo = (a - hi.astype(F32)).astype(BF16)
    return hi, lo


def stacked(a):
    hi = a.astype(BF16).astype(F32)
    return jnp.concatenate([hi, a - hi], axis=0).astype(BF16)


def mm(a, b):
    return lax.dot_general(a, b, (((1,), (0,)), ((), ())), preferred_element_type=F32)


def mm_t(a, b):
    return lax.dot_general(a, b, (((1,), (1,)), ((), ())), preferred_element_type=F32)


def halves(a):
    n = a.shape[0] // 2
    return a[:n] + a[n:]


def kernel(rs_hbm, u_hbm, v_hbm, c_hbm, out_ref, r0, u, v, cpl, cur_t,
           l0, rc0, r0s, lx, rcx, rxs, l1, rc1, r1s, lb, rcb, rbs,
           px, slb, zbr, ybr, x1, xb, x1h, x1l, xbh, xbl,
           p0, q0r, p1, q1p, p2, q2p, q2s, p3, q3p, q3s, p4, q4p,
           wall, ld, ss, rs):
    y = lax.axis_index("grp")
    s = lax.axis_index("sub")
    core = s % 2
    chip = (s // 2) % 8
    plane = s // 16
    lane = s % 16
    base = s - lane

    def near(k):
        return (y, base + (lane + k) % 16)

    def same_core(k):
        return (y, base + 2 * ((chip + k) % 8) + core)

    other_core = (y, s + 1 - 2 * core)
    plane_by = {1: plane + 1 - 2 * (plane % 2), 2: (plane + 2) % 4, 3: 3 - plane}
    y2 = y + 2 - 4 * ((y // 2) % 2)
    y_by = {1: y + 1 - 2 * (y % 2), 2: y2, 3: 4 * (y // 4) + 3 - y % 4, 4: (y + 4) % 8, 6: (y2 + 4) % 8}

    def far(zmask, ymask):
        ss_ = s + 16 * (plane_by[zmask] - plane) if zmask else s
        return (y_by[ymask] if ymask else y, ss_)

    far_masks = [(1, 0), (2, 0), (3, 0), (0, 1), (1, 1), (2, 1), (3, 1), (0, 2), (0, 3), (0, 4), (0, 6)]
    MESH = pl.DeviceIdType.MESH
    barrier = pltpu.get_barrier_semaphore()
    for m in far_masks:
        pl.semaphore_signal(barrier, inc=1, device_id=far(*m), device_id_type=MESH)
    for k in range(1, 16):
        pl.semaphore_signal(barrier, inc=1, device_id=near(k), device_id_type=MESH)

    loads = {}

    def load(name, src, dst):
        loads[name] = pltpu.make_async_copy(src, dst, ld.at[len(loads)])
        loads[name].start()

    load("r", rs_hbm, r0)
    for name in ("v0", "u0", "v1", "c0", "u2", "v3", "v4", "u3", "c1", "u1", "v2", "c2", "c3", "c4", "u4"):
        src, dst = {"u": (u_hbm, u), "v": (v_hbm, v), "c": (c_hbm, cpl)}[name[0]]
        load(name, src.at[int(name[1])], dst.at[int(name[1])])

    pending = []
    count = [0]

    def send(copies, total):
        i = count[0]
        count[0] += 1

        def copy(src, dst, device):
            return pltpu.make_async_remote_copy(src_ref=src, dst_ref=dst, send_sem=ss.at[i], recv_sem=rs.at[i],
                                                device_id=device, device_id_type=MESH)

        for one in copies:
            copy(*one).start()
        cp = copy(total, total, copies[0][2])
        pending.append(cp)
        return cp

    def flush():
        for cp in old + pending:
            cp.wait_send()

    old = []

    def flush_old():
        for cp in old:
            cp.wait_send()
        old[:] = pending
        pending.clear()

    def core_send(l, rc):
        return send([(l.at[1 - core], rc, other_core)], rc)

    def core_add(cp, l, rc):
        cp.wait_recv()
        rc[...] = rc[...] + l[core]

    def rs_send(rc, slots):
        return send([(rc.at[(chip + k) % 8], slots.at[k - 1], same_core(k)) for k in range(1, 8)], slots)

    def rs_sum(cp, rc, slots):
        cp.wait_recv()
        total = rc[chip]
        for k in range(7):
            total = total + slots[k]
        return total

    def ag_send(full, first=0, size=XS):
        own = full.at[core, chip, pl.ds(first, size)]
        return send([(own, own, same_core(k)) for k in range(1, 8)], full.at[core, pl.ds(0, 7), pl.ds(first, size)])

    def share_send(cp, full, first=0, size=XS):
        cp.wait_recv()
        rows = pl.ds(first, size)
        return send([(full.at[core, i, rows], full.at[core, i, rows], other_core) for i in range(8)],
                    full.at[1 - core, pl.ds(0, 8), rows])

    def all_send(src, slots, masks):
        return send([(src, slots.at[i], far(*m)) for i, m in enumerate(masks)], slots)

    def w_send(level, value):
        mine = wall.at[level, core * 8 + chip]
        mine[...] = value
        return send([(mine, mine, near(k)) for k in range(1, 16)], wall.at[level, pl.ds(0, 15)])

    def w_full(level, cp):
        cp.wait_recv()
        return stacked(wall[level].reshape(COLS, RANK))

    def weights(level, own, sibling, upper):
        loads["c%d" % level].wait()
        first = jnp.where(upper == 0, own, sibling)
        second = jnp.where(upper == 0, sibling, own)
        node = jnp.concatenate([first, second], axis=1)
        return halves(mm_t(stacked(node), cpl[level]))

    def slices(value, n):
        return value.reshape(2, 8, n, RANK)

    def product(w_s, hi, lo):
        return halves(mm(w_s, hi)) + mm(w_s, lo)[:SL]

    def split_full(full, his, los, first, last):
        for i in range(first, last):
            hi, lo = split2(full[:, :, i * XS:(i + 1) * XS, :].reshape(RANK, RANK))
            his[i], los[i] = hi, lo

    bit4, bit5 = plane % 2, plane // 2
    planes = [(1, 0), (2, 0), (3, 0)]
    w_cps = {}

    loads["r"].wait()
    rt = r0[...].T
    cur_t[...] = rt
    rts = stacked(rt)
    loads["v0"].wait()
    l0[...] = slices(halves(mm(rts, v[0])), SL)
    pl.semaphore_wait(barrier, len(far_masks) + 15)
    c_0 = core_send(l0, rc0)
    loads["v1"].wait()
    loads["u0"].wait()
    lx[:, :, 0:SL, :] = slices(halves(mm(rts, v[1])), SL)
    lx[:, :, SL:SL + XS, :] = slices(mm(u[0].T, v[1]), XS)
    c_x = core_send(lx, rcx)
    core_add(c_0, l0, rc0)
    g_0 = rs_send(rc0, r0s)
    core_add(c_x, lx, rcx)
    g_x = rs_send(rcx, rxs)
    loads["u2"].wait()
    loads["v3"].wait()
    loads["v4"].wait()
    ut = u[2].T
    for i, m in enumerate((3, 4)):
        lb[:, :, i * XS:(i + 1) * XS, :] = slices(mm(ut, v[m]), XS)
    loads["u3"].wait()
    ut = u[3].T
    lb[:, :, 2 * XS:3 * XS, :] = slices(mm(ut, v[4]), XS)
    c_b = core_send(lb, rcb)
    p0[...] = rs_sum(g_0, rc0, r0s)
    e_0 = all_send(p0, q0r, [(1, 0)])
    px[...] = rs_sum(g_x, rcx, rxs)
    x1[core, chip] = px[SL:SL + XS]
    a_x = ag_send(x1)
    core_add(c_b, lb, rcb)
    e_0.wait_recv()
    w_0 = weights(0, p0[...], q0r[0], bit4)
    ws = stacked(w_0)
    w_cps[0] = w_send(0, w_0)
    g_b = rs_send(rcb, rbs)
    s_x = share_send(a_x, x1)
    s_x.wait_recv()
    split_full(x1, x1h, x1l, 0, 1)
    p1[...] = px[0:SL] - product(ws, x1h[0], x1l[0])
    e_1 = all_send(p1, q1p, planes)
    w0 = w_full(0, w_cps[0])
    cur_t[...] = cur_t[...] - halves(mm_t(w0, u[0]))
    upd = mm_t(u[0], w0)
    out_ref[...] = r0[...] - (upd[:, :COLS] + upd[:, COLS:])

    def apply(level, ws_=None):
        if ws_ is None:
            ws_ = w_full(level, w_cps[level])
        if level == 4:
            loads["u4"].wait()
        upd_ = mm_t(u[level], ws_)
        out_ref[...] = out_ref[...] - (upd_[:, :COLS] + upd_[:, COLS:])

    slb[...] = rs_sum(g_b, rcb, rbs)
    z_b = all_send(slb, zbr, planes)

    e_1.wait_recv()
    w_cps[1] = w_send(1, weights(1, p1[...] + q1p[0], q1p[1] + q1p[2], bit5))

    loads["u1"].wait()
    loads["v2"].wait()
    w1 = w_full(1, w_cps[1])
    cur_s = stacked(cur_t[...] - halves(mm_t(w1, u[1])))
    for m in (2, 3, 4):
        l1[:, :, (m - 2) * SL:(m - 1) * SL, :] = slices(halves(mm(cur_s, v[m])), SL)
    c_1 = core_send(l1, rc1)
    core_add(c_1, l1, rc1)
    g_1 = rs_send(rc1, r1s)
    z_b.wait_recv()
    xb[core, chip] = slb[...] + zbr[0] + (zbr[1] + zbr[2])
    y_b = all_send(xb.at[core, chip, pl.ds(2 * XS, XS)], ybr, [(0, 1)])
    a_b = ag_send(xb, 0, 2 * XS)
    p2[...] = rs_sum(g_1, rc1, r1s)
    peers = [(1, 0), (2, 0), (3, 0), (0, 1), (1, 1), (2, 1), (3, 1)]
    e_2 = all_send(p2.at[pl.ds(0, SL)], q2p, peers)
    e_2s = all_send(p2.at[pl.ds(SL, 2 * SL)], q2s, planes)
    flush_old()
    y_b.wait_recv()
    y_b.wait_send()
    old[:] = [cp for cp in old if cp is not y_b]
    xb[core, chip, pl.ds(2 * XS, XS)] = xb[core, chip, pl.ds(2 * XS, XS)] + ybr[0]
    a_c = ag_send(xb, 2 * XS, XS)
    s_b = share_send(a_b, xb, 0, 2 * XS)
    apply(1, w1)

    e_2.wait_recv()
    w = weights(2, (p2[0:SL] + q2p[0]) + (q2p[1] + q2p[2]), (q2p[3] + q2p[4]) + (q2p[5] + q2p[6]), y % 2)
    e_2s.wait_recv()
    rest = (p2[SL:3 * SL] + q2s[0]) + (q2s[1] + q2s[2])
    s_b.wait_recv()
    split_full(xb, xbh, xbl, 0, 2)
    ws = stacked(w)
    for i in range(2):
        p3[i * SL:(i + 1) * SL] = rest[i * SL:(i + 1) * SL] - product(ws, xbh[i], xbl[i])
    e_3 = all_send(p3.at[pl.ds(0, SL)], q3p, [(0, 1), (0, 2), (0, 3)])
    e_3s = all_send(p3.at[pl.ds(SL, SL)], q3s, [(0, 1)])
    w_cps[2] = w_send(2, w)
    flush_old()
    s_c = share_send(a_c, xb, 2 * XS, XS)
    apply(2)
    s_c.wait_recv()
    split_full(xb, xbh, xbl, 2, 3)

    e_3.wait_recv()
    w = weights(3, p3[0:SL] + q3p[0], q3p[1] + q3p[2], (y // 2) % 2)
    e_3s.wait_recv()
    p4[...] = p3[SL:2 * SL] + q3s[0] - product(stacked(w), xbh[2], xbl[2])
    e_4 = all_send(p4, q4p, [(0, 2), (0, 4), (0, 6)])
    flush_old()
    w_cps[3] = w_send(3, w)
    apply(3)

    e_4.wait_recv()
    w = weights(4, p4[...] + q4p[0], q4p[1] + q4p[2], y // 4)
    w_cps[4] = w_send(4, w)
    apply(4)
    flush()


def per_device(right_sides, basis_u, basis_v, coupling):
    def vm(*shape, dtype=F32):
        return pltpu.VMEM(shape, dtype)

    scratch = [
        vm(PTS, COLS), vm(LEVELS, PTS, RANK, dtype=BF16), vm(LEVELS, PTS, RANK, dtype=BF16),
        vm(LEVELS, RANK, 2 * RANK, dtype=BF16), vm(COLS, PTS),
    ]
    for n in (SL, SL + XS, 3 * SL, 3 * XS):
        scratch += [vm(2, 8, n, RANK), vm(8, n, RANK), vm(7, n, RANK)]
    scratch += [
        vm(SL + XS, RANK), vm(3 * XS, RANK), vm(3, 3 * XS, RANK), vm(1, XS, RANK),
        vm(2, 8, XS, RANK), vm(2, 8, 3 * XS, RANK),
    ]
    scratch += [vm(1, RANK, RANK, dtype=BF16)] * 2 + [vm(3, RANK, RANK, dtype=BF16)] * 2
    scratch += [
        vm(SL, RANK), vm(1, SL, RANK),
        vm(SL, RANK), vm(3, SL, RANK),
        vm(3 * SL, RANK), vm(7, SL, RANK), vm(3, 2 * SL, RANK),
        vm(2 * SL, RANK), vm(3, SL, RANK), vm(1, SL, RANK),
        vm(SL, RANK), vm(3, SL, RANK),
        vm(LEVELS, 16, SL, RANK),
        pltpu.SemaphoreType.DMA((16,)), pltpu.SemaphoreType.DMA((SEMS,)), pltpu.SemaphoreType.DMA((SEMS,)),
    ]
    return pl.pallas_call(
        kernel,
        out_shape=jax.ShapeDtypeStruct((PTS, COLS), F32),
        in_specs=[pl.BlockSpec(memory_space=pltpu.HBM)] * 4,
        out_specs=pl.BlockSpec(memory_space=pltpu.VMEM),
        scratch_shapes=scratch,
        compiler_params=pltpu.CompilerParams(collective_id=0, has_side_effects=True, vmem_limit_bytes=60 * 2**20),
        name="hodlr_solve",
    )(right_sides, basis_u, basis_v, coupling)


def solution(mesh):
    in_specs = (
        P(("grp", "sub"), None),
        P(None, ("grp", "sub"), None),
        P(None, ("grp", "sub"), None),
        P(None, ("grp", "sub"), None),
    )
    out_specs = P(("grp", "sub"), None)
    return jax.shard_map(
        per_device, mesh=mesh, in_specs=in_specs, out_specs=out_specs, check_vma=False
    )
```

```python
import functools

import jax
import jax.numpy as jnp
from jax import lax
from jax.experimental import pallas as pl
from jax.experimental.pallas import tpu as pltpu
from jax.sharding import PartitionSpec as P

F32 = jnp.float32
BF16 = jnp.bfloat16
RANK = 256
PTS = 512
COLS = 128
LEVELS = 5
SEMS = 29
SL = 8
XS = 16


def split2(a):
    hi = a.astype(BF16)
    lo = (a - hi.astype(F32)).astype(BF16)
    return hi, lo


def stacked(a):
    hi = a.astype(BF16).astype(F32)
    return jnp.concatenate([hi, a - hi], axis=0).astype(BF16)


def mm(a, b):
    return lax.dot_general(a, b, (((1,), (0,)), ((), ())), preferred_element_type=F32)


def mm_t(a, b):
    return lax.dot_general(a, b, (((1,), (1,)), ((), ())), preferred_element_type=F32)


def halves(a):
    n = a.shape[0] // 2
    return a[:n] + a[n:]


def kernel(rs_hbm, u_hbm, v_hbm, c_hbm, out_ref, r0, u, v, cpl, cur_t,
           l0, rc0, r0s, lx, rcx, rxs, l1, rc1, r1s, lb, rcb, rbs,
           px, slb, zbr, ybr, x1, xb, x1h, x1l, xbh, xbl,
           q0r, p1, q1p, p2, q2p, q2s, p3, q3p, q3s, p4, q4p,
           wall, ld, ss, rs):
    y = lax.axis_index("grp")
    s = lax.axis_index("sub")
    core = s % 2
    chip = (s // 2) % 8
    plane = s // 16
    lane = s % 16
    base = s - lane

    def near(k):
        c = (core + k % 2) % 2
        return (y, base + 2 * chip_at(k // 2) + c)

    def chip_at(k):
        return 4 * ((chip // 4 + k % 2) % 2) + (chip % 4 + k // 2) % 4

    def same_core(k):
        return (y, base + 2 * chip_at(k) + core)

    chips = (5, 4, 3, 7, 2, 6, 1)
    devices = [2 * k + c for k in chips for c in (0, 1)] + [1]

    other_core = (y, s + 1 - 2 * core)
    plane_by = {1: plane + 1 - 2 * (plane % 2), 2: (plane + 2) % 4, 3: 3 - plane}
    y2 = y + 2 - 4 * ((y // 2) % 2)
    y_by = {1: y + 1 - 2 * (y % 2), 2: y2, 3: 4 * (y // 4) + 3 - y % 4, 4: (y + 4) % 8, 6: (y2 + 4) % 8}

    def far(zmask, ymask):
        ss_ = s + 16 * (plane_by[zmask] - plane) if zmask else s
        return (y_by[ymask] if ymask else y, ss_)

    def hops(zmask, ymask):
        return (0, 2, 4, 2)[zmask] + (0, 1, 2, 3, 4, 0, 2)[ymask]

    far_masks = [(1, 0), (2, 0), (3, 0), (0, 1), (1, 1), (2, 1), (3, 1), (0, 2), (0, 3), (0, 4), (0, 6)]
    MESH = pl.DeviceIdType.MESH
    barrier = pltpu.get_barrier_semaphore()
    for m in sorted(far_masks, key=lambda m: -hops(*m)):
        pl.semaphore_signal(barrier, inc=1, device_id=far(*m), device_id_type=MESH)
    for k in devices:
        pl.semaphore_signal(barrier, inc=1, device_id=near(k), device_id_type=MESH)

    loads = {}

    def load(name, src, dst):
        loads[name] = pltpu.make_async_copy(src, dst, ld.at[len(loads)])
        loads[name].start()

    def load_all(names):
        for name in names:
            load_one(name)

    def load_one(name):
        if name == "r":
            load(name, rs_hbm, r0)
        else:
            src, dst = {"u": (u_hbm, u), "v": (v_hbm, v), "c": (c_hbm, cpl)}[name[0]]
            load(name, src.at[int(name[1])], dst.at[int(name[1])])

    load_all(("r", "v0", "v1", "u0"))
    pending = []
    count = [0]

    def send(copies, total):
        i = count[0]
        count[0] += 1

        def copy(src, dst, device):
            return pltpu.make_async_remote_copy(src_ref=src, dst_ref=dst, send_sem=ss.at[i], recv_sem=rs.at[i],
                                                device_id=device, device_id_type=MESH)

        for one in copies:
            copy(*one).start()
        cp = copy(total, total, copies[0][2])
        pending.append(cp)
        return cp

    def flush():
        for cp in old + pending:
            cp.wait_send()

    old = []

    def flush_old():
        for cp in old:
            cp.wait_send()
        old[:] = pending
        pending.clear()

    def core_send(l, rc):
        return send([(l.at[1 - core], rc, other_core)], rc)

    def core_add(cp, l, rc):
        cp.wait_recv()
        rc[...] = rc[...] + l[core]

    def rs_send(rc, slots):
        return send([(rc.at[chip_at(k)], slots.at[k - 1], same_core(k)) for k in chips], slots)

    def rs_sum(cp, rc, slots):
        cp.wait_recv()
        total = rc[chip]
        for k in range(7):
            total = total + slots[k]
        return total

    def ag_send(full, first=0, size=XS):
        own = full.at[core, chip, pl.ds(first, size)]
        return send([(own, own, same_core(k)) for k in chips], full.at[core, pl.ds(0, 7), pl.ds(first, size)])

    def share_send(cp, full, first=0, size=XS):
        cp.wait_recv()
        rows = pl.ds(first, size)
        return send([(full.at[core, i, rows], full.at[core, i, rows], other_core) for i in range(8)],
                    full.at[1 - core, pl.ds(0, 8), rows])

    def all_send(src, slots, masks):
        order = sorted(range(len(masks)), key=lambda i: -hops(*masks[i]))
        return send([(src, slots.at[i], far(*masks[i])) for i in order], slots)

    def w_send(level, value):
        mine = wall.at[level, core * 8 + chip]
        mine[...] = value
        return send([(mine, mine, near(k)) for k in devices], wall.at[level, pl.ds(0, 15)])

    def w_full(level, cp):
        cp.wait_recv()
        return stacked(wall[level].reshape(COLS, RANK))

    def weights(level, own, sibling, upper):
        loads["c%d" % level].wait()
        first = jnp.where(upper == 0, own, sibling)
        second = jnp.where(upper == 0, sibling, own)
        node = jnp.concatenate([first, second], axis=1)
        return halves(mm_t(stacked(node), cpl[level]))

    def slices(value, n):
        return value.reshape(2, 8, n, RANK)

    def product(w_s, hi, lo):
        return halves(mm(w_s, hi)) + mm(w_s, lo)[:SL]

    def split_full(full, his, los, first, last):
        for i in range(first, last):
            hi, lo = split2(full[:, :, i * XS:(i + 1) * XS, :].reshape(RANK, RANK))
            his[i], los[i] = hi, lo

    bit4, bit5 = plane % 2, plane // 2
    planes = [(1, 0), (2, 0), (3, 0)]
    w_cps = {}

    loads["r"].wait()
    rt = r0[...].T
    cur_t[...] = rt
    rts = stacked(rt)
    loads["v0"].wait()
    l0[:, :, 0:SL, :] = slices(halves(mm(rts, v[0])), SL)
    loads["v1"].wait()
    l0[:, :, SL:2 * SL, :] = slices(halves(mm(rts, v[1])), SL)
    pl.semaphore_wait(barrier, len(far_masks) + 15)
    c_0 = core_send(l0, rc0)
    loads["u0"].wait()
    load_all(("u2", "v3", "v4", "u3", "c0", "u1", "v2", "c1", "c2", "c3", "c4", "u4"))
    lx[...] = slices(mm(u[0].T, v[1]), XS)
    c_x = core_send(lx, rcx)
    core_add(c_0, l0, rc0)
    g_0 = rs_send(rc0, r0s)
    core_add(c_x, lx, rcx)
    g_x = rs_send(rcx, rxs)
    loads["u2"].wait()
    loads["v3"].wait()
    loads["v4"].wait()
    ut = u[2].T
    for i, m in enumerate((3, 4)):
        lb[:, :, i * XS:(i + 1) * XS, :] = slices(mm(ut, v[m]), XS)
    loads["u3"].wait()
    ut = u[3].T
    lb[:, :, 2 * XS:3 * XS, :] = slices(mm(ut, v[4]), XS)
    c_b = core_send(lb, rcb)
    px[...] = rs_sum(g_0, rc0, r0s)
    e_0 = all_send(px.at[pl.ds(0, SL)], q0r, [(1, 0)])
    x1[core, chip] = rs_sum(g_x, rcx, rxs)
    a_x = ag_send(x1)
    core_add(c_b, lb, rcb)
    e_0.wait_recv()
    w_0 = weights(0, px[0:SL], q0r[0], bit4)
    ws = stacked(w_0)
    w_cps[0] = w_send(0, w_0)
    g_b = rs_send(rcb, rbs)
    s_x = share_send(a_x, x1)
    s_x.wait_recv()
    split_full(x1, x1h, x1l, 0, 1)
    p1[...] = px[SL:2 * SL] - product(ws, x1h[0], x1l[0])
    e_1 = all_send(p1, q1p, planes)
    w0 = w_full(0, w_cps[0])
    cur_t[...] = cur_t[...] - halves(mm_t(w0, u[0]))
    upd = mm_t(u[0], w0)
    out_ref[...] = r0[...] - (upd[:, :COLS] + upd[:, COLS:])

    def apply(level, ws_=None):
        if ws_ is None:
            ws_ = w_full(level, w_cps[level])
        if level == 4:
            loads["u4"].wait()
        upd_ = mm_t(u[level], ws_)
        out_ref[...] = out_ref[...] - (upd_[:, :COLS] + upd_[:, COLS:])

    slb[...] = rs_sum(g_b, rcb, rbs)
    z_b = all_send(slb, zbr, planes)

    e_1.wait_recv()
    w_cps[1] = w_send(1, weights(1, p1[...] + q1p[0], q1p[1] + q1p[2], bit5))

    loads["u1"].wait()
    loads["v2"].wait()
    w1 = w_full(1, w_cps[1])
    cur_s = stacked(cur_t[...] - halves(mm_t(w1, u[1])))
    for m in (2, 3, 4):
        l1[:, :, (m - 2) * SL:(m - 1) * SL, :] = slices(halves(mm(cur_s, v[m])), SL)
    c_1 = core_send(l1, rc1)
    core_add(c_1, l1, rc1)
    g_1 = rs_send(rc1, r1s)
    z_b.wait_recv()
    xb[core, chip] = slb[...] + zbr[0] + (zbr[1] + zbr[2])
    y_b = all_send(xb.at[core, chip, pl.ds(2 * XS, XS)], ybr, [(0, 1)])
    a_b = ag_send(xb, 0, 2 * XS)
    p2[...] = rs_sum(g_1, rc1, r1s)
    peers = [(1, 0), (2, 0), (3, 0), (0, 1), (1, 1), (2, 1), (3, 1)]
    e_2 = all_send(p2.at[pl.ds(0, SL)], q2p, peers)
    e_2s = all_send(p2.at[pl.ds(SL, 2 * SL)], q2s, planes)
    flush_old()
    y_b.wait_recv()
    y_b.wait_send()
    old[:] = [cp for cp in old if cp is not y_b]
    xb[core, chip, pl.ds(2 * XS, XS)] = xb[core, chip, pl.ds(2 * XS, XS)] + ybr[0]
    a_c = ag_send(xb, 2 * XS, XS)
    s_b = share_send(a_b, xb, 0, 2 * XS)
    apply(1, w1)

    e_2.wait_recv()
    w = weights(2, (p2[0:SL] + q2p[0]) + (q2p[1] + q2p[2]), (q2p[3] + q2p[4]) + (q2p[5] + q2p[6]), y % 2)
    e_2s.wait_recv()
    rest = (p2[SL:3 * SL] + q2s[0]) + (q2s[1] + q2s[2])
    s_b.wait_recv()
    split_full(xb, xbh, xbl, 0, 2)
    ws = stacked(w)
    for i in range(2):
        p3[i * SL:(i + 1) * SL] = rest[i * SL:(i + 1) * SL] - product(ws, xbh[i], xbl[i])
    e_3 = all_send(p3.at[pl.ds(0, SL)], q3p, [(0, 1), (0, 2), (0, 3)])
    e_3s = all_send(p3.at[pl.ds(SL, SL)], q3s, [(0, 1)])
    w_cps[2] = w_send(2, w)
    flush_old()
    s_c = share_send(a_c, xb, 2 * XS, XS)
    apply(2)
    s_c.wait_recv()
    split_full(xb, xbh, xbl, 2, 3)

    e_3.wait_recv()
    w = weights(3, p3[0:SL] + q3p[0], q3p[1] + q3p[2], (y // 2) % 2)
    e_3s.wait_recv()
    p4[...] = p3[SL:2 * SL] + q3s[0] - product(stacked(w), xbh[2], xbl[2])
    e_4 = all_send(p4, q4p, [(0, 2), (0, 4), (0, 6)])
    flush_old()
    w_cps[3] = w_send(3, w)
    apply(3)

    e_4.wait_recv()
    w = weights(4, p4[...] + q4p[0], q4p[1] + q4p[2], y // 4)
    w_cps[4] = w_send(4, w)
    apply(4)
    flush()


def per_device(right_sides, basis_u, basis_v, coupling):
    def vm(*shape, dtype=F32):
        return pltpu.VMEM(shape, dtype)

    scratch = [
        vm(PTS, COLS), vm(LEVELS, PTS, RANK, dtype=BF16), vm(LEVELS, PTS, RANK, dtype=BF16),
        vm(LEVELS, RANK, 2 * RANK, dtype=BF16), vm(COLS, PTS),
    ]
    for n in (2 * SL, XS, 3 * SL, 3 * XS):
        scratch += [vm(2, 8, n, RANK), vm(8, n, RANK), vm(7, n, RANK)]
    scratch += [
        vm(2 * SL, RANK), vm(3 * XS, RANK), vm(3, 3 * XS, RANK), vm(1, XS, RANK),
        vm(2, 8, XS, RANK), vm(2, 8, 3 * XS, RANK),
    ]
    scratch += [vm(1, RANK, RANK, dtype=BF16)] * 2 + [vm(3, RANK, RANK, dtype=BF16)] * 2
    scratch += [
        vm(1, SL, RANK),
        vm(SL, RANK), vm(3, SL, RANK),
        vm(3 * SL, RANK), vm(7, SL, RANK), vm(3, 2 * SL, RANK),
        vm(2 * SL, RANK), vm(3, SL, RANK), vm(1, SL, RANK),
        vm(SL, RANK), vm(3, SL, RANK),
        vm(LEVELS, 16, SL, RANK),
        pltpu.SemaphoreType.DMA((16,)), pltpu.SemaphoreType.DMA((SEMS,)), pltpu.SemaphoreType.DMA((SEMS,)),
    ]
    return pl.pallas_call(
        kernel,
        out_shape=jax.ShapeDtypeStruct((PTS, COLS), F32),
        in_specs=[pl.BlockSpec(memory_space=pltpu.HBM)] * 4,
        out_specs=pl.BlockSpec(memory_space=pltpu.VMEM),
        scratch_shapes=scratch,
        compiler_params=pltpu.CompilerParams(collective_id=0, has_side_effects=True, vmem_limit_bytes=int(53.5 * 2**20)),
        name="hodlr_solve",
    )(right_sides, basis_u, basis_v, coupling)


def solution(mesh):
    in_specs = (
        P(("grp", "sub"), None),
        P(None, ("grp", "sub"), None),
        P(None, ("grp", "sub"), None),
        P(None, ("grp", "sub"), None),
    )
    out_specs = P(("grp", "sub"), None)
    return jax.shard_map(
        per_device, mesh=mesh, in_specs=in_specs, out_specs=out_specs, check_vma=False
    )
```

```python
import functools

import jax
import jax.numpy as jnp
from jax import lax
from jax.experimental import pallas as pl
from jax.experimental.pallas import tpu as pltpu
from jax.sharding import PartitionSpec as P

F32 = jnp.float32
BF16 = jnp.bfloat16
RANK = 256
PTS = 512
COLS = 128
LEVELS = 5
SEMS = 30
SL = 8
XS = 16


def split2(a):
    hi = a.astype(BF16)
    lo = (a - hi.astype(F32)).astype(BF16)
    return hi, lo


def stacked(a):
    hi = a.astype(BF16).astype(F32)
    return jnp.concatenate([hi, a - hi], axis=0).astype(BF16)


def mm(a, b):
    return lax.dot_general(a, b, (((1,), (0,)), ((), ())), preferred_element_type=F32)


def mm_t(a, b):
    return lax.dot_general(a, b, (((1,), (1,)), ((), ())), preferred_element_type=F32)


def halves(a):
    n = a.shape[0] // 2
    return a[:n] + a[n:]


def kernel(rs_hbm, u_hbm, v_hbm, c_hbm, out_ref, r0, u, v, cpl, cur_t,
           l0, rc0, r0s, lx, rcx, rxs, l1, rc1, r1s, l2, rc2, r2s, lb, rcb, rbs,
           px, slb, zbr, ybr, x1, xb, x1h, x1l, xbh, xbl,
           q0r, p1, q1p, p2, q2p, q2s, p3, q3p, q3s, p4, q4p,
           wall, wpair, ld, ss, rs):
    y = lax.axis_index("grp")
    s = lax.axis_index("sub")
    core = s % 2
    chip = (s // 2) % 8
    plane = s // 16
    lane = s % 16
    base = s - lane

    def near(k):
        c = (core + k % 2) % 2
        return (y, base + 2 * chip_at(k // 2) + c)

    def chip_at(k):
        return 4 * ((chip // 4 + k % 2) % 2) + (chip % 4 + k // 2) % 4

    def same_core(k):
        return (y, base + 2 * chip_at(k) + core)

    chips = (5, 4, 3, 7, 2, 6, 1)
    devices = [2 * k + c for k in chips for c in (0, 1)] + [1]

    other_core = (y, s + 1 - 2 * core)
    plane_by = {1: plane + 1 - 2 * (plane % 2), 2: (plane + 2) % 4, 3: 3 - plane}
    y2 = y + 2 - 4 * ((y // 2) % 2)
    y_by = {1: y + 1 - 2 * (y % 2), 2: y2, 3: 4 * (y // 4) + 3 - y % 4, 4: (y + 4) % 8, 6: (y2 + 4) % 8}

    def far(zmask, ymask):
        ss_ = s + 16 * (plane_by[zmask] - plane) if zmask else s
        return (y_by[ymask] if ymask else y, ss_)

    def far_other(zmask, ymask):
        y_, s_ = far(zmask, ymask)
        return (y_, s_ + 1 - 2 * core)

    both = [(1, 0), (2, 0), (3, 0), (0, 2), (0, 4), (0, 6)]

    def hops(zmask, ymask):
        return (0, 2, 4, 2)[zmask] + (0, 1, 2, 3, 4, 0, 2)[ymask]

    far_masks = [(1, 0), (2, 0), (3, 0), (0, 1), (1, 1), (2, 1), (3, 1), (0, 2), (0, 3), (0, 4), (0, 6)]
    MESH = pl.DeviceIdType.MESH
    barrier = pltpu.get_barrier_semaphore()
    for m in sorted(far_masks, key=lambda m: -hops(*m)):
        pl.semaphore_signal(barrier, inc=1, device_id=far(*m), device_id_type=MESH)
    for m in both:
        pl.semaphore_signal(barrier, inc=1, device_id=far_other(*m), device_id_type=MESH)
    for k in devices:
        pl.semaphore_signal(barrier, inc=1, device_id=near(k), device_id_type=MESH)

    loads = {}

    def load(name, src, dst):
        loads[name] = pltpu.make_async_copy(src, dst, ld.at[len(loads)])
        loads[name].start()

    def load_all(names):
        for name in names:
            load_one(name)

    def load_one(name):
        if name == "r":
            load(name, rs_hbm, r0)
        else:
            src, dst = {"u": (u_hbm, u), "v": (v_hbm, v), "c": (c_hbm, cpl)}[name[0]]
            load(name, src.at[int(name[1])], dst.at[int(name[1])])

    load_all(("r", "v0", "v1", "u0"))
    pending = []
    count = [0]

    def send(copies, total):
        i = count[0]
        count[0] += 1

        def copy(src, dst, device):
            return pltpu.make_async_remote_copy(src_ref=src, dst_ref=dst, send_sem=ss.at[i], recv_sem=rs.at[i],
                                                device_id=device, device_id_type=MESH)

        for one in copies:
            copy(*one).start()
        cp = copy(total, total, copies[0][2])
        pending.append(cp)
        return cp

    def flush():
        for cp in old + pending:
            cp.wait_send()

    old = []

    def flush_old():
        for cp in old:
            cp.wait_send()
        old[:] = pending
        pending.clear()

    def core_send(l, rc):
        return send([(l.at[1 - core], rc, other_core)], rc)

    def core_add(cp, l, rc):
        cp.wait_recv()
        rc[...] = rc[...] + l[core]

    def rs_send(rc, slots):
        return send([(rc.at[chip_at(k)], slots.at[k - 1], same_core(k)) for k in chips], slots)

    def rs_sum(cp, rc, slots):
        cp.wait_recv()
        total = rc[chip]
        for k in range(7):
            total = total + slots[k]
        return total

    def ag_send(full, first=0, size=XS):
        own = full.at[core, chip, pl.ds(first, size)]
        return send([(own, own, same_core(k)) for k in chips], full.at[core, pl.ds(0, 7), pl.ds(first, size)])

    def share_send(cp, full, first=0, size=XS):
        cp.wait_recv()
        rows = pl.ds(first, size)
        return send([(full.at[core, i, rows], full.at[core, i, rows], other_core) for i in range(8)],
                    full.at[1 - core, pl.ds(0, 8), rows])

    def all_send(src, slots, masks):
        order = sorted(range(len(masks)), key=lambda i: -hops(*masks[i]))
        return send([(src, slots.at[i], far(*masks[i])) for i in order], slots)

    def w_send(level, value):
        mine = wall.at[level, core * 8 + chip]
        mine[...] = value
        return send([(mine, mine, near(k)) for k in devices], wall.at[level, pl.ds(0, 15)])

    def pair_send(src, slots, masks):
        slots[4 * core] = src[...]
        order = sorted(range(len(masks)), key=lambda i: -hops(*masks[i]))
        copies = [(src, slots.at[4 * core + 1 + i], to(*masks[i])) for i in order for to in (far, far_other)]
        return send(copies + [(src, slots.at[4 * core], other_core)], slots.at[pl.ds(0, 7)])

    def pair_weights(level, q, upper):
        own = jnp.concatenate([q[0] + q[1], q[4] + q[5]], axis=0)
        sibling = jnp.concatenate([q[2] + q[3], q[6] + q[7]], axis=0)
        return weights(level, own, sibling, upper)

    def pair_w_send(i, value):
        wpair[i, 0, chip] = value[:SL]
        wpair[i, 1, chip] = value[SL:]
        mine = wpair.at[i, pl.ds(0, 2), chip]
        return send([(mine, mine, same_core(k)) for k in chips], wpair.at[i, pl.ds(0, 2), pl.ds(0, 7)])

    def w_full(level, cp):
        cp.wait_recv()
        if level in (1, 4):
            return stacked(wpair[level // 4].reshape(COLS, RANK))
        return stacked(wall[level].reshape(COLS, RANK))

    def weights(level, own, sibling, upper):
        loads["c%d" % level].wait()
        first = jnp.where(upper == 0, own, sibling)
        second = jnp.where(upper == 0, sibling, own)
        node = jnp.concatenate([first, second], axis=1)
        return halves(mm_t(stacked(node), cpl[level]))

    def slices(value, n):
        return value.reshape(2, 8, n, RANK)

    def product(w_s, hi, lo):
        return halves(mm(w_s, hi)) + mm(w_s, lo)[:SL]

    def split_full(full, his, los, first, last):
        for i in range(first, last):
            hi, lo = split2(full[:, :, i * XS:(i + 1) * XS, :].reshape(RANK, RANK))
            his[i], los[i] = hi, lo

    bit4, bit5 = plane % 2, plane // 2
    planes = [(1, 0), (2, 0), (3, 0)]
    w_cps = {}

    loads["r"].wait()
    rt = r0[...].T
    cur_t[...] = rt
    rts = stacked(rt)
    loads["v0"].wait()
    l0[:, :, 0:SL, :] = slices(halves(mm(rts, v[0])), SL)
    loads["v1"].wait()
    l0[:, :, SL:2 * SL, :] = slices(halves(mm(rts, v[1])), SL)
    pl.semaphore_wait(barrier, len(far_masks) + len(both) + 15)
    c_0 = core_send(l0, rc0)
    loads["u0"].wait()
    load_all(("u2", "v3", "v4", "u3", "c0", "u1", "v2", "c1", "c2", "c3", "c4", "u4"))
    lx[...] = slices(mm(u[0].T, v[1]), XS)
    c_x = core_send(lx, rcx)
    core_add(c_0, l0, rc0)
    g_0 = rs_send(rc0, r0s)
    core_add(c_x, lx, rcx)
    g_x = rs_send(rcx, rxs)
    loads["u2"].wait()
    loads["v3"].wait()
    loads["v4"].wait()
    ut = u[2].T
    for i, m in enumerate((3, 4)):
        lb[:, :, i * XS:(i + 1) * XS, :] = slices(mm(ut, v[m]), XS)
    loads["u3"].wait()
    ut = u[3].T
    lb[:, :, 2 * XS:3 * XS, :] = slices(mm(ut, v[4]), XS)
    c_b = core_send(lb, rcb)
    px[...] = rs_sum(g_0, rc0, r0s)
    e_0 = all_send(px.at[pl.ds(0, SL)], q0r, [(1, 0)])
    x1[core, chip] = rs_sum(g_x, rcx, rxs)
    a_x = ag_send(x1)
    core_add(c_b, lb, rcb)
    e_0.wait_recv()
    w_0 = weights(0, px[0:SL], q0r[0], bit4)
    ws = stacked(w_0)
    w_cps[0] = w_send(0, w_0)
    g_b = rs_send(rcb, rbs)
    s_x = share_send(a_x, x1)
    s_x.wait_recv()
    split_full(x1, x1h, x1l, 0, 1)
    p1[...] = px[SL:2 * SL] - product(ws, x1h[0], x1l[0])
    e_1 = pair_send(p1, q1p, planes)
    w0 = w_full(0, w_cps[0])
    cur_t[...] = cur_t[...] - halves(mm_t(w0, u[0]))
    upd = mm_t(u[0], w0)
    out_ref[...] = r0[...] - (upd[:, :COLS] + upd[:, COLS:])

    def apply(level, ws_=None):
        if ws_ is None:
            ws_ = w_full(level, w_cps[level])
        if level == 4:
            loads["u4"].wait()
        upd_ = mm_t(u[level], ws_)
        out_ref[...] = out_ref[...] - (upd_[:, :COLS] + upd_[:, COLS:])

    slb[...] = rs_sum(g_b, rcb, rbs)
    z_b = all_send(slb, zbr, planes)

    e_1.wait_recv()
    w_cps[1] = pair_w_send(0, pair_weights(1, q1p, bit5))

    loads["u1"].wait()
    loads["v2"].wait()
    w1 = w_full(1, w_cps[1])
    cur_s = stacked(cur_t[...] - halves(mm_t(w1, u[1])))
    l1[...] = slices(halves(mm(cur_s, v[2])), SL)
    c_1 = core_send(l1, rc1)
    for m in (3, 4):
        l2[:, :, (m - 3) * SL:(m - 2) * SL, :] = slices(halves(mm(cur_s, v[m])), SL)
    c_2 = core_send(l2, rc2)
    core_add(c_1, l1, rc1)
    g_1 = rs_send(rc1, r1s)
    core_add(c_2, l2, rc2)
    g_2 = rs_send(rc2, r2s)
    z_b.wait_recv()
    xb[core, chip] = slb[...] + zbr[0] + (zbr[1] + zbr[2])
    y_b = all_send(xb.at[core, chip, pl.ds(2 * XS, XS)], ybr, [(0, 1)])
    a_b = ag_send(xb, 0, 2 * XS)
    p2[0:SL] = rs_sum(g_1, rc1, r1s)
    peers = [(1, 0), (2, 0), (3, 0), (0, 1), (1, 1), (2, 1), (3, 1)]
    e_2 = all_send(p2.at[pl.ds(0, SL)], q2p, peers)
    p2[SL:3 * SL] = rs_sum(g_2, rc2, r2s)
    e_2s = all_send(p2.at[pl.ds(SL, 2 * SL)], q2s, planes)
    flush_old()
    y_b.wait_recv()
    y_b.wait_send()
    old[:] = [cp for cp in old if cp is not y_b]
    xb[core, chip, pl.ds(2 * XS, XS)] = xb[core, chip, pl.ds(2 * XS, XS)] + ybr[0]
    a_c = ag_send(xb, 2 * XS, XS)
    s_b = share_send(a_b, xb, 0, 2 * XS)
    apply(1, w1)

    e_2.wait_recv()
    w = weights(2, (p2[0:SL] + q2p[0]) + (q2p[1] + q2p[2]), (q2p[3] + q2p[4]) + (q2p[5] + q2p[6]), y % 2)
    e_2s.wait_recv()
    rest = (p2[SL:3 * SL] + q2s[0]) + (q2s[1] + q2s[2])
    s_b.wait_recv()
    split_full(xb, xbh, xbl, 0, 2)
    ws = stacked(w)
    for i in range(2):
        p3[i * SL:(i + 1) * SL] = rest[i * SL:(i + 1) * SL] - product(ws, xbh[i], xbl[i])
    e_3 = all_send(p3.at[pl.ds(0, SL)], q3p, [(0, 1), (0, 2), (0, 3)])
    e_3s = all_send(p3.at[pl.ds(SL, SL)], q3s, [(0, 1)])
    w_cps[2] = w_send(2, w)
    flush_old()
    s_c = share_send(a_c, xb, 2 * XS, XS)
    apply(2)
    s_c.wait_recv()
    split_full(xb, xbh, xbl, 2, 3)

    e_3.wait_recv()
    w = weights(3, p3[0:SL] + q3p[0], q3p[1] + q3p[2], (y // 2) % 2)
    e_3s.wait_recv()
    p4[...] = p3[SL:2 * SL] + q3s[0] - product(stacked(w), xbh[2], xbl[2])
    e_4 = pair_send(p4, q4p, [(0, 2), (0, 4), (0, 6)])
    flush_old()
    w_cps[3] = w_send(3, w)
    apply(3)

    e_4.wait_recv()
    w_cps[4] = pair_w_send(1, pair_weights(4, q4p, y // 4))
    apply(4)
    flush()


def per_device(right_sides, basis_u, basis_v, coupling):
    def vm(*shape, dtype=F32):
        return pltpu.VMEM(shape, dtype)

    scratch = [
        vm(PTS, COLS), vm(LEVELS, PTS, RANK, dtype=BF16), vm(LEVELS, PTS, RANK, dtype=BF16),
        vm(LEVELS, RANK, 2 * RANK, dtype=BF16), vm(COLS, PTS),
    ]
    for n in (2 * SL, XS, SL, 2 * SL, 3 * XS):
        scratch += [vm(2, 8, n, RANK), vm(8, n, RANK), vm(7, n, RANK)]
    scratch += [
        vm(2 * SL, RANK), vm(3 * XS, RANK), vm(3, 3 * XS, RANK), vm(1, XS, RANK),
        vm(2, 8, XS, RANK), vm(2, 8, 3 * XS, RANK),
    ]
    scratch += [vm(1, RANK, RANK, dtype=BF16)] * 2 + [vm(3, RANK, RANK, dtype=BF16)] * 2
    scratch += [
        vm(1, SL, RANK),
        vm(SL, RANK), vm(8, SL, RANK),
        vm(3 * SL, RANK), vm(7, SL, RANK), vm(3, 2 * SL, RANK),
        vm(2 * SL, RANK), vm(3, SL, RANK), vm(1, SL, RANK),
        vm(SL, RANK), vm(8, SL, RANK),
        vm(LEVELS, 16, SL, RANK), vm(2, 2, 8, SL, RANK),
        pltpu.SemaphoreType.DMA((16,)), pltpu.SemaphoreType.DMA((SEMS,)), pltpu.SemaphoreType.DMA((SEMS,)),
    ]
    return pl.pallas_call(
        kernel,
        out_shape=jax.ShapeDtypeStruct((PTS, COLS), F32),
        in_specs=[pl.BlockSpec(memory_space=pltpu.HBM)] * 4,
        out_specs=pl.BlockSpec(memory_space=pltpu.VMEM),
        scratch_shapes=scratch,
        compiler_params=pltpu.CompilerParams(collective_id=0, has_side_effects=True, vmem_limit_bytes=int(53.5 * 2**20)),
        name="hodlr_solve",
    )(right_sides, basis_u, basis_v, coupling)


def solution(mesh):
    in_specs = (
        P(("grp", "sub"), None),
        P(None, ("grp", "sub"), None),
        P(None, ("grp", "sub"), None),
        P(None, ("grp", "sub"), None),
    )
    out_specs = P(("grp", "sub"), None)
    return jax.shard_map(
        per_device, mesh=mesh, in_specs=in_specs, out_specs=out_specs, check_vma=False
    )
```

```python
import functools

import jax
import jax.numpy as jnp
from jax import lax
from jax.experimental import pallas as pl
from jax.experimental.pallas import tpu as pltpu
from jax.sharding import PartitionSpec as P

F32 = jnp.float32
BF16 = jnp.bfloat16
RANK = 256
PTS = 512
COLS = 128
LEVELS = 5
SEMS = 30
SL = 8
XS = 16


def split2(a):
    hi = a.astype(BF16)
    lo = (a - hi.astype(F32)).astype(BF16)
    return hi, lo


def stacked(a):
    hi = a.astype(BF16).astype(F32)
    return jnp.concatenate([hi, a - hi], axis=0).astype(BF16)


def mm(a, b):
    return lax.dot_general(a, b, (((1,), (0,)), ((), ())), preferred_element_type=F32)


def mm_t(a, b):
    return lax.dot_general(a, b, (((1,), (1,)), ((), ())), preferred_element_type=F32)


def halves(a):
    n = a.shape[0] // 2
    return a[:n] + a[n:]


def kernel(rs_hbm, u_hbm, v_hbm, c_hbm, out_ref, r0, u, v, cpl, cur_t,
           l0, rc0, r0s, lx, rcx, rxs, l1, rc1, r1s, l2, rc2, r2s, lb, rcb, rbs,
           px, slb, zbr, ybr, x1, xb, x1h, x1l, xbh, xbl,
           q0r, p1, q1p, p2, q2p, q2s, p3, q3p, q3s, p4, q4p,
           wall, wpair, ld, ss, rs):
    y = lax.axis_index("grp")
    s = lax.axis_index("sub")
    core = s % 2
    chip = (s // 2) % 8
    plane = s // 16
    lane = s % 16
    base = s - lane

    def near(k):
        c = (core + k % 2) % 2
        return (y, base + 2 * chip_at(k // 2) + c)

    def chip_at(k):
        return 4 * ((chip // 4 + k % 2) % 2) + (chip % 4 + k // 2) % 4

    def same_core(k):
        return (y, base + 2 * chip_at(k) + core)

    chips = (5, 4, 3, 7, 2, 6, 1)
    devices = [2 * k + c for k in chips for c in (0, 1)] + [1]

    other_core = (y, s + 1 - 2 * core)
    plane_by = {1: plane + 1 - 2 * (plane % 2), 2: (plane + 2) % 4, 3: 3 - plane}
    y2 = y + 2 - 4 * ((y // 2) % 2)
    y_by = {1: y + 1 - 2 * (y % 2), 2: y2, 3: 4 * (y // 4) + 3 - y % 4, 4: (y + 4) % 8, 6: (y2 + 4) % 8}

    def far(zmask, ymask):
        ss_ = s + 16 * (plane_by[zmask] - plane) if zmask else s
        return (y_by[ymask] if ymask else y, ss_)

    def far_other(zmask, ymask):
        y_, s_ = far(zmask, ymask)
        return (y_, s_ + 1 - 2 * core)

    both = [(1, 0), (2, 0), (3, 0), (0, 2), (0, 4), (0, 6)]

    def hops(zmask, ymask):
        return (0, 2, 4, 2)[zmask] + (0, 1, 2, 3, 4, 0, 2)[ymask]

    far_masks = [(1, 0), (2, 0), (3, 0), (0, 1), (1, 1), (2, 1), (3, 1), (0, 2), (0, 3), (0, 4), (0, 6)]
    MESH = pl.DeviceIdType.MESH
    barrier = pltpu.get_barrier_semaphore()
    for m in sorted(far_masks, key=lambda m: -hops(*m)):
        pl.semaphore_signal(barrier, inc=1, device_id=far(*m), device_id_type=MESH)
    for m in both:
        pl.semaphore_signal(barrier, inc=1, device_id=far_other(*m), device_id_type=MESH)
    for k in devices:
        pl.semaphore_signal(barrier, inc=1, device_id=near(k), device_id_type=MESH)

    loads = {}

    def load(name, src, dst):
        loads[name] = pltpu.make_async_copy(src, dst, ld.at[len(loads)])
        loads[name].start()

    def load_all(names):
        for name in names:
            load_one(name)

    def load_one(name):
        if name == "r":
            load(name, rs_hbm, r0)
        else:
            src, dst = {"u": (u_hbm, u), "v": (v_hbm, v), "c": (c_hbm, cpl)}[name[0]]
            load(name, src.at[int(name[1])], dst.at[int(name[1])])

    load_all(("r", "v0", "v1", "u0"))
    pending = []
    count = [0]

    def send(copies, total):
        i = count[0]
        count[0] += 1

        def copy(src, dst, device):
            return pltpu.make_async_remote_copy(src_ref=src, dst_ref=dst, send_sem=ss.at[i], recv_sem=rs.at[i],
                                                device_id=device, device_id_type=MESH)

        for one in copies:
            copy(*one).start()
        cp = copy(total, total, copies[0][2])
        pending.append(cp)
        return cp

    def flush():
        for cp in old + pending:
            cp.wait_send()

    old = []

    def flush_old():
        for cp in old:
            cp.wait_send()
        old[:] = pending
        pending.clear()

    def core_send(l, rc):
        return send([(l.at[1 - core], rc, other_core)], rc)

    def core_add(cp, l, rc):
        cp.wait_recv()
        rc[...] = rc[...] + l[core]

    def rs_send(rc, slots):
        return send([(rc.at[chip_at(k)], slots.at[k - 1], same_core(k)) for k in chips], slots)

    def rs_sum(cp, rc, slots):
        cp.wait_recv()
        total = rc[chip]
        for k in range(7):
            total = total + slots[k]
        return total

    def ag_send(full, first=0, size=XS):
        own = full.at[core, chip, pl.ds(first, size)]
        return send([(own, own, same_core(k)) for k in chips], full.at[core, pl.ds(0, 7), pl.ds(first, size)])

    def share_send(cp, full, first=0, size=XS):
        cp.wait_recv()
        rows = pl.ds(first, size)
        return send([(full.at[core, i, rows], full.at[core, i, rows], other_core) for i in range(8)],
                    full.at[1 - core, pl.ds(0, 8), rows])

    def all_send(src, slots, masks):
        order = sorted(range(len(masks)), key=lambda i: -hops(*masks[i]))
        return send([(src, slots.at[i], far(*masks[i])) for i in order], slots)

    def w_send(level, value):
        mine = wall.at[level, core * 8 + chip]
        mine[...] = value
        return send([(mine, mine, near(k)) for k in devices], wall.at[level, pl.ds(0, 15)])

    def pair_send(src, slots, masks):
        slots[4 * core] = src[...]
        order = sorted(range(len(masks)), key=lambda i: -hops(*masks[i]))
        copies = [(src, slots.at[4 * core + 1 + i], to(*masks[i])) for i in order for to in (far, far_other)]
        return send(copies + [(src, slots.at[4 * core], other_core)], slots.at[pl.ds(0, 7)])

    def pair_weights(level, q, upper):
        own = jnp.concatenate([q[0] + q[1], q[4] + q[5]], axis=0)
        sibling = jnp.concatenate([q[2] + q[3], q[6] + q[7]], axis=0)
        return weights(level, own, sibling, upper)

    def pair_w_send(i, value):
        wpair[i, 0, chip] = value[:SL]
        wpair[i, 1, chip] = value[SL:]
        mine = wpair.at[i, pl.ds(0, 2), chip]
        return send([(mine, mine, same_core(k)) for k in chips], wpair.at[i, pl.ds(0, 2), pl.ds(0, 7)])

    def w_full(level, cp):
        cp.wait_recv()
        if level in (1, 4):
            return stacked(wpair[level // 4].reshape(COLS, RANK))
        return stacked(wall[level].reshape(COLS, RANK))

    def weights(level, own, sibling, upper):
        loads["c%d" % level].wait()
        first = jnp.where(upper == 0, own, sibling)
        second = jnp.where(upper == 0, sibling, own)
        node = jnp.concatenate([first, second], axis=1)
        return halves(mm_t(stacked(node), cpl[level]))

    def slices(value, n):
        return value.reshape(2, 8, n, RANK)

    def product(w_s, hi, lo):
        return halves(mm(w_s, hi)) + mm(w_s, lo)[:SL]

    def split_full(full, his, los, first, last):
        for i in range(first, last):
            hi, lo = split2(full[:, :, i * XS:(i + 1) * XS, :].reshape(RANK, RANK))
            his[i], los[i] = hi, lo

    bit4, bit5 = plane % 2, plane // 2
    planes = [(1, 0), (2, 0), (3, 0)]
    w_cps = {}

    loads["r"].wait()
    rt = r0[...].T
    cur_t[...] = rt
    rts = stacked(rt)
    loads["v0"].wait()
    l0[:, :, 0:SL, :] = slices(halves(mm(rts, v[0])), SL)
    loads["v1"].wait()
    l0[:, :, SL:2 * SL, :] = slices(halves(mm(rts, v[1])), SL)
    pl.semaphore_wait(barrier, len(far_masks) + len(both) + 15)
    c_0 = core_send(l0, rc0)
    loads["u0"].wait()
    load_all(("u2", "v3", "v4", "u3", "c0", "u1", "v2", "c1", "c2", "c3", "c4", "u4"))
    lx[...] = slices(mm(u[0].T, v[1]), XS)
    c_x = core_send(lx, rcx)
    core_add(c_0, l0, rc0)
    g_0 = rs_send(rc0, r0s)
    core_add(c_x, lx, rcx)
    g_x = rs_send(rcx, rxs)
    loads["u2"].wait()
    loads["v3"].wait()
    loads["v4"].wait()
    ut = u[2].T
    for i, m in enumerate((3, 4)):
        lb[:, :, i * XS:(i + 1) * XS, :] = slices(mm(ut, v[m]), XS)
    loads["u3"].wait()
    ut = u[3].T
    lb[:, :, 2 * XS:3 * XS, :] = slices(mm(ut, v[4]), XS)
    c_b = core_send(lb, rcb)
    px[...] = rs_sum(g_0, rc0, r0s)
    e_0 = all_send(px.at[pl.ds(0, SL)], q0r, [(1, 0)])
    x1[core, chip] = rs_sum(g_x, rcx, rxs)
    a_x = ag_send(x1)
    core_add(c_b, lb, rcb)
    g_b = rs_send(rcb, rbs)
    e_0.wait_recv()
    w_0 = weights(0, px[0:SL], q0r[0], bit4)
    ws = stacked(w_0)
    w_cps[0] = w_send(0, w_0)
    s_x = share_send(a_x, x1)
    s_x.wait_recv()
    split_full(x1, x1h, x1l, 0, 1)
    p1[...] = px[SL:2 * SL] - product(ws, x1h[0], x1l[0])
    e_1 = pair_send(p1, q1p, planes)
    w0 = w_full(0, w_cps[0])
    cur_t[...] = cur_t[...] - halves(mm_t(w0, u[0]))
    upd = mm_t(u[0], w0)
    out_ref[...] = r0[...] - (upd[:, :COLS] + upd[:, COLS:])

    def apply(level, ws_=None):
        if ws_ is None:
            ws_ = w_full(level, w_cps[level])
        if level == 4:
            loads["u4"].wait()
        upd_ = mm_t(u[level], ws_)
        out_ref[...] = out_ref[...] - (upd_[:, :COLS] + upd_[:, COLS:])

    slb[...] = rs_sum(g_b, rcb, rbs)
    z_b = all_send(slb, zbr, planes)

    e_1.wait_recv()
    w_cps[1] = pair_w_send(0, pair_weights(1, q1p, bit5))

    loads["u1"].wait()
    loads["v2"].wait()
    w1 = w_full(1, w_cps[1])
    cur_s = stacked(cur_t[...] - halves(mm_t(w1, u[1])))
    l1[...] = slices(halves(mm(cur_s, v[2])), SL)
    c_1 = core_send(l1, rc1)
    for m in (3, 4):
        l2[:, :, (m - 3) * SL:(m - 2) * SL, :] = slices(halves(mm(cur_s, v[m])), SL)
    c_2 = core_send(l2, rc2)
    core_add(c_1, l1, rc1)
    g_1 = rs_send(rc1, r1s)
    core_add(c_2, l2, rc2)
    g_2 = rs_send(rc2, r2s)
    z_b.wait_recv()
    xb[core, chip] = slb[...] + zbr[0] + (zbr[1] + zbr[2])
    y_b = all_send(xb.at[core, chip, pl.ds(2 * XS, XS)], ybr, [(0, 1)])
    a_b = ag_send(xb, 0, 2 * XS)
    p2[0:SL] = rs_sum(g_1, rc1, r1s)
    peers = [(1, 0), (2, 0), (3, 0), (0, 1), (1, 1), (2, 1), (3, 1)]
    e_2 = all_send(p2.at[pl.ds(0, SL)], q2p, peers)
    p2[SL:3 * SL] = rs_sum(g_2, rc2, r2s)
    e_2s = all_send(p2.at[pl.ds(SL, 2 * SL)], q2s, planes)
    flush_old()
    y_b.wait_recv()
    y_b.wait_send()
    old[:] = [cp for cp in old if cp is not y_b]
    xb[core, chip, pl.ds(2 * XS, XS)] = xb[core, chip, pl.ds(2 * XS, XS)] + ybr[0]
    a_c = ag_send(xb, 2 * XS, XS)
    s_b = share_send(a_b, xb, 0, 2 * XS)
    apply(1, w1)

    e_2.wait_recv()
    w = weights(2, (p2[0:SL] + q2p[0]) + (q2p[1] + q2p[2]), (q2p[3] + q2p[4]) + (q2p[5] + q2p[6]), y % 2)
    e_2s.wait_recv()
    rest = (p2[SL:3 * SL] + q2s[0]) + (q2s[1] + q2s[2])
    s_b.wait_recv()
    split_full(xb, xbh, xbl, 0, 2)
    ws = stacked(w)
    for i in range(2):
        p3[i * SL:(i + 1) * SL] = rest[i * SL:(i + 1) * SL] - product(ws, xbh[i], xbl[i])
    e_3 = all_send(p3.at[pl.ds(0, SL)], q3p, [(0, 1), (0, 2), (0, 3)])
    e_3s = all_send(p3.at[pl.ds(SL, SL)], q3s, [(0, 1)])
    w_cps[2] = w_send(2, w)
    flush_old()
    s_c = share_send(a_c, xb, 2 * XS, XS)
    apply(2)
    s_c.wait_recv()
    split_full(xb, xbh, xbl, 2, 3)

    e_3.wait_recv()
    w = weights(3, p3[0:SL] + q3p[0], q3p[1] + q3p[2], (y // 2) % 2)
    e_3s.wait_recv()
    p4[...] = p3[SL:2 * SL] + q3s[0] - product(stacked(w), xbh[2], xbl[2])
    e_4 = pair_send(p4, q4p, [(0, 2), (0, 4), (0, 6)])
    flush_old()
    w_cps[3] = w_send(3, w)
    apply(3)

    e_4.wait_recv()
    w_cps[4] = pair_w_send(1, pair_weights(4, q4p, y // 4))
    apply(4)
    flush()


def per_device(right_sides, basis_u, basis_v, coupling):
    def vm(*shape, dtype=F32):
        return pltpu.VMEM(shape, dtype)

    scratch = [
        vm(PTS, COLS), vm(LEVELS, PTS, RANK, dtype=BF16), vm(LEVELS, PTS, RANK, dtype=BF16),
        vm(LEVELS, RANK, 2 * RANK, dtype=BF16), vm(COLS, PTS),
    ]
    for n in (2 * SL, XS, SL, 2 * SL, 3 * XS):
        scratch += [vm(2, 8, n, RANK), vm(8, n, RANK), vm(7, n, RANK)]
    scratch += [
        vm(2 * SL, RANK), vm(3 * XS, RANK), vm(3, 3 * XS, RANK), vm(1, XS, RANK),
        vm(2, 8, XS, RANK), vm(2, 8, 3 * XS, RANK),
    ]
    scratch += [vm(1, RANK, RANK, dtype=BF16)] * 2 + [vm(3, RANK, RANK, dtype=BF16)] * 2
    scratch += [
        vm(1, SL, RANK),
        vm(SL, RANK), vm(8, SL, RANK),
        vm(3 * SL, RANK), vm(7, SL, RANK), vm(3, 2 * SL, RANK),
        vm(2 * SL, RANK), vm(3, SL, RANK), vm(1, SL, RANK),
        vm(SL, RANK), vm(8, SL, RANK),
        vm(LEVELS, 16, SL, RANK), vm(2, 2, 8, SL, RANK),
        pltpu.SemaphoreType.DMA((16,)), pltpu.SemaphoreType.DMA((SEMS,)), pltpu.SemaphoreType.DMA((SEMS,)),
    ]
    return pl.pallas_call(
        kernel,
        out_shape=jax.ShapeDtypeStruct((PTS, COLS), F32),
        in_specs=[pl.BlockSpec(memory_space=pltpu.HBM)] * 4,
        out_specs=pl.BlockSpec(memory_space=pltpu.VMEM),
        scratch_shapes=scratch,
        compiler_params=pltpu.CompilerParams(collective_id=0, has_side_effects=True, vmem_limit_bytes=int(53.5 * 2**20)),
        name="hodlr_solve",
    )(right_sides, basis_u, basis_v, coupling)


def solution(mesh):
    in_specs = (
        P(("grp", "sub"), None),
        P(None, ("grp", "sub"), None),
        P(None, ("grp", "sub"), None),
        P(None, ("grp", "sub"), None),
    )
    out_specs = P(("grp", "sub"), None)
    return jax.shard_map(
        per_device, mesh=mesh, in_specs=in_specs, out_specs=out_specs, check_vma=False
    )
```
